512 devices in a mesh: ctx: 64 (over x, y, z_lo), head: 8 (over z_hi, core).
Axes of the slice: x: 4, y: 4, z: 16 (z_hi: 4, z_lo: 4; z = z_hi * 4 + z_lo), core: 2. Of those that a mesh axis runs over, the one named last changes fastest.
Arguments:
- hidden: bfloat16 [8192, 7168], P('ctx', 'head'), may hold values from -6 to 6
- w_dkv: bfloat16 [7168, 576], P('head'), may hold values from -0.0625 to 0.0625
- kv_gain: float32 [512], replicated, may hold values from 0.25 to 1.75
- w_uk: bfloat16 [512, 6144], P(None, 'head'), may hold values from -0.25 to 0.25
- w_uv: bfloat16 [512, 6144], P(None, 'head'), may hold values from -0.25 to 0.25
- queries: bfloat16 [8192, 9216], P('ctx', 'head'), may hold values from -140 to 140
- segments: int32 [8192], P('ctx'), may hold values from 0 to 2, as said below
- positions: int32 [8192], P('ctx'), may hold values from 0 to 6143, as said below
Outputs:
- attended: bfloat16 [8192, 6144], P('ctx', 'head')
The draws below stay inside these ranges and needn't reach their ends.
Inputs may be any that keep to these rules, and one draw needn't show every extreme that they name: `segments`: 0 marks the shared video prompt, 1 the chosen caption, 2 the rejected caption; ids never fall along the sequence; the prompt holds 2048 to 4096 tokens, one of the two captions exactly 2048 tokens and the other the rest. `positions`: a token's index in the sequence for the prompt and the chosen caption; for the rejected caption its index minus the chosen caption's length, so that it continues the prompt.
All inputs are finite; a program needn't handle non-finite values.
Results may differ from the reference program's by a relative error of at most 0.012.
The reference program's roundings to bfloat16 on the way count: a program that leaves them out, or rounds other values in their place, can miss the bound.
Values may be sent and summed in bfloat16 or wider, within the bound.
A program may use at most 64 MiB of HBM per device.

```python
import math
import jax
import jax.numpy as jnp
from jax import lax

D = 7168
KVL = 512
RD = 64
NOPE = 128
VD = 128
HEADS = 48
TOKENS = 8192


def pair_bounds(key):
    first_key, second_key = jax.random.split(key)
    prompt_end = jax.random.randint(first_key, (), TOKENS // 4, TOKENS // 2 + 1)
    longer = TOKENS - TOKENS // 4 - prompt_end
    chosen_longer = jax.random.randint(second_key, (), 0, 2)
    chosen_length = jnp.where(chosen_longer == 1, longer, TOKENS // 4)
    return (prompt_end, prompt_end + chosen_length)


def draw_segments(key, part):
    prompt_end, chosen_end = pair_bounds(key)
    token_index = jnp.arange(TOKENS, dtype=jnp.int32)
    return (token_index >= prompt_end).astype(jnp.int32) + (token_index >= chosen_end).astype(jnp.int32)


def draw_positions(key, part):
    prompt_end, chosen_end = pair_bounds(key)
    token_index = jnp.arange(TOKENS, dtype=jnp.int32)
    return jnp.where(token_index >= chosen_end, token_index - (chosen_end - prompt_end), token_index).astype(jnp.int32)


def draw_queries(key, part):
    key = jax.random.fold_in(key, 3)
    array_shape = (TOKENS, HEADS * (NOPE + RD))
    values = 2.5 * jax.random.normal(key, array_shape, jnp.float32)
    return jnp.clip(values, -12.0, 12.0).astype(jnp.bfloat16)


def levels(key, extent, cuts, smallest, largest):
    loudness = 1.0
    for position, shards_of in cuts:
        heights = jax.random.uniform(jax.random.fold_in(jax.random.fold_in(key, 6), position), (shards_of,), jnp.float32, smallest / len(cuts), largest / len(cuts))
        loudness = loudness * jnp.repeat(jnp.exp(heights), extent[position] // shards_of).reshape((-1,) + (1,) * (len(extent) - 1 - position))
    return loudness


def scatter_about(key, extent, width, most, cuts=(), kind=jnp.bfloat16):
    entries = width * jax.random.normal(key, extent, jnp.float32)
    if cuts:
        entries = entries * levels(key, extent, cuts, -0.22, 0.18)
    return jnp.clip(entries, -most, most).astype(kind)


def setup_inputs(seed: int = 0) -> dict:
    arg_keys = jax.random.split(jax.random.key(seed), 9)
    return {
        "hidden": scatter_about(arg_keys[0], (TOKENS, D), 1.0, 6.0, ((0, 64), (1, 8))),
        "w_dkv": scatter_about(arg_keys[1], (D, KVL + RD), D ** -0.5, 0.0625, ((0, 8),)),
        "kv_gain": jnp.clip(1.0 + 0.15 * jax.random.normal(arg_keys[2], (KVL,), jnp.float32), 0.25, 1.75),
        "w_uk": scatter_about(arg_keys[3], (KVL, HEADS * NOPE), KVL ** -0.5, 0.25, ((1, 8),)),
        "w_uv": scatter_about(arg_keys[4], (KVL, HEADS * VD), KVL ** -0.5, 0.25, ((1, 8),)),
        "queries": draw_queries(jax.random.fold_in(arg_keys[8], 71), 0),
        "segments": draw_segments(jax.random.fold_in(arg_keys[8], 71), 0),
        "positions": draw_positions(jax.random.fold_in(arg_keys[8], 71), 0),
    }


ROPE_BASE = 10000.0
NORM_EPS = 1e-06

def rotary(values, positions):
    half_width = values.shape[-1] // 2
    frequency = jnp.exp(jnp.arange(half_width, dtype=jnp.float32) * (-2.0 * math.log(ROPE_BASE) / values.shape[-1]))
    angles = positions.astype(jnp.float32)[..., None] * frequency
    cosine = jnp.cos(angles)
    sine_part = jnp.sin(angles)
    first_half = values[..., :half_width]
    second = values[..., half_width:]
    return jnp.concatenate([first_half * cosine - second * sine_part, second * cosine + first_half * sine_part], axis=-1)

def finish_keys(latent, positions, kv_gain):
    compressed = latent[:, :KVL]
    mean_square = lax.optimization_barrier(jnp.mean(compressed * compressed, axis=-1, keepdims=True))
    normed = (compressed * lax.rsqrt(mean_square + NORM_EPS) * kv_gain).astype(jnp.bfloat16)
    rope_part = rotary(latent[:, KVL:], positions).astype(jnp.bfloat16)
    return jnp.concatenate([normed, rope_part], axis=-1)

def reference(hidden, w_dkv, kv_gain, w_uk, w_uv, queries, segments, positions):
    latent = jnp.dot(hidden, w_dkv, preferred_element_type=jnp.float32)
    key_rows = finish_keys(latent, positions, kv_gain)
    head_count = w_uk.shape[1] // NOPE
    score_scale = 1.0 / math.sqrt(NOPE + RD)
    shaped = queries.reshape(TOKENS, head_count, NOPE + RD)
    query_rope = rotary(shaped[:, :, NOPE:].astype(jnp.float32), positions[:, None]).astype(jnp.bfloat16)
    absorbed = jnp.einsum('rhn,khn->rhk', shaped[:, :, :NOPE].astype(jnp.float32), w_uk.reshape(KVL, head_count, NOPE).astype(jnp.float32)).astype(jnp.bfloat16)
    query_full = jnp.concatenate([absorbed, query_rope], axis=-1)
    block_rows = 256 if TOKENS % 256 == 0 else TOKENS
    key_index = jnp.arange(TOKENS, dtype=jnp.int32)
    all_keys = key_rows.astype(jnp.float32)
    compressed_keys = all_keys[:, :KVL]
    value_weight = w_uv.reshape(KVL, head_count, VD).astype(jnp.float32)

    def one_block(block_index):
        first_row = (block_index * block_rows).astype(jnp.int32)
        block_query = lax.dynamic_slice_in_dim(query_full, first_row, block_rows, 0).astype(jnp.float32)
        query_index = first_row + jnp.arange(block_rows, dtype=jnp.int32)
        query_segment = lax.dynamic_slice_in_dim(segments, first_row, block_rows, 0)
        visible = (key_index[None, :] <= query_index[:, None]) & ((segments[None, :] == query_segment[:, None]) | (segments[None, :] == 0))
        visible_mask = visible[:, None, :]
        scores = jnp.einsum('rhk,nk->rhn', block_query, all_keys) * score_scale
        top_score = lax.optimization_barrier(jnp.max(jnp.where(visible_mask, scores, -jnp.inf), axis=-1, keepdims=True))
        weights = jnp.where(visible_mask, jnp.exp(scores - top_score), 0.0)
        weight_sum = lax.optimization_barrier(jnp.sum(weights, axis=-1, keepdims=True))
        rounded = lax.optimization_barrier(weights.astype(jnp.bfloat16)).astype(jnp.float32)
        mixture = jnp.einsum('rhn,nk->rhk', rounded, compressed_keys) / weight_sum
        mixed_latent = mixture.astype(jnp.bfloat16).astype(jnp.float32)
        return jnp.einsum('rhk,khv->rhv', mixed_latent, value_weight).astype(jnp.bfloat16)
    outputs = lax.map(one_block, jnp.arange(TOKENS // block_rows, dtype=jnp.int32))
    return outputs.reshape(TOKENS, head_count * VD)
```

```python
import functools
import math

import jax
import jax.numpy as jnp
from jax import lax
from jax.experimental import pallas as pl
from jax.experimental.pallas import tpu as pltpu
from jax.sharding import PartitionSpec as P

KVL = 512
RD = 64
NOPE = 128
VD = 128
ROPE_BASE = 10000.0
NORM_EPS = 1e-06
ROWS = 128
HEADS = 6
HIDDEN_MASK = -1e30
EXP_SCALE = math.log2(math.e) / math.sqrt(NOPE + RD)
MESH = pl.DeviceIdType.MESH
NT = (((1,), (1,)), ((), ()))
RING = (1, 3, 2)


def place(x, y, z, core):
    x, y, z = (x + 8) % 4, (y + 8) % 4, (z + 32) % 16
    return (x * 16 + y * 4 + z % 4, (z // 4) * 2 + core)


def remote(src, dst, send, recv, device):
    return pltpu.make_async_remote_copy(
        src_ref=src, dst_ref=dst, send_sem=send, recv_sem=recv, device_id=device, device_id_type=MESH
    )


def rope_tables(pos):
    lane = lax.broadcasted_iota(jnp.int32, (1, RD), 1)
    half = (lane % (RD // 2)).astype(jnp.float32)
    frequency = jnp.exp(half * (-2.0 * math.log(ROPE_BASE) / RD))
    angles = pos.astype(jnp.float32) * frequency
    sign = jnp.where(lane < RD // 2, -1.0, 1.0)
    return jnp.cos(angles), jnp.sin(angles) * sign


def rotate(v, cosine, sine):
    swapped = jnp.concatenate([v[:, RD // 2 :], v[:, : RD // 2]], axis=1)
    return v * cosine + swapped * sine


def kernel(
    hid_ref, wd_ref, gain_ref, wuk_ref, wuv_ref, q_ref, pos_ref, seg_ref, out_ref,
    lat_send, lat_recv, tot, rs_recv, key_a, key_b, key_c, qf, acc, m_s, l_s,
    s_sib, r_sib, s_rs, r_rs, s_ag, r_ag, s_p1, r_p1, s_p2, r_p2, s_p3, r_p3, s_hf, r_hf, s_sh, r_sh,
):
    ctx, head = lax.axis_index("ctx"), lax.axis_index("head")
    x, y, zl = ctx // 16, (ctx // 4) % 4, ctx % 4
    zh, c = head // 2, head % 2
    z = zh * 4 + zl
    sib = place(x, y, z, 1 - c)
    f32, bf16 = jnp.float32, jnp.bfloat16

    barrier = pltpu.get_barrier_semaphore()
    offsets = [(1, 0, 0), (2, 0, 0), (3, 0, 0), (0, 1, 0), (0, 2, 0), (0, 3, 0)]
    offsets += [(0, 0, k) for k in (1, -1, 2, -2, 4, 8, 12)]
    pl.semaphore_signal(barrier, inc=1, device_id=sib, device_id_type=MESH)
    for dx, dy, dz in offsets:
        pl.semaphore_signal(barrier, inc=1, device_id=place(x + dx, y + dy, z + dz, c), device_id_type=MESH)

    def partial(first):
        return jnp.dot(hid_ref[pl.ds(first, 64), :], wd_ref[...], preferred_element_type=f32)

    other = pl.multiple_of((1 - c) * 64, 64)
    mine = pl.multiple_of(c * 64, 64)
    lat_send[:, KVL + RD :] = jnp.zeros((64, 64), f32)
    lat_send[:, : KVL + RD] = partial(other)
    pl.semaphore_wait(barrier, 1 + len(offsets))
    swap = remote(lat_send, lat_recv, s_sib, r_sib, sib)
    swap.start()
    own = jnp.concatenate([partial(mine), jnp.zeros((64, 64), f32)], axis=1)
    swap.wait()
    tot[...] = (own + lat_recv[...]).reshape(4, 16, 640)

    rs = [
        remote(tot.at[(zh + k) % 4], rs_recv.at[k - 1], s_rs.at[k - 1], r_rs.at[k - 1], place(x, y, z + 4 * k, c))
        for k in (1, 2, 3)
    ]
    for copy in rs:
        copy.start()

    cos_q, sin_q = rope_tables(pos_ref[...])
    hide = jnp.where(seg_ref[...] == 2, HIDDEN_MASK, 0.0).astype(bf16)
    lane = lax.broadcasted_iota(jnp.int32, (ROWS, RD), 1)
    feature = jnp.where(lane == 0, hide.astype(f32), 0.0)
    for h in range(HEADS):
        base = h * (NOPE + RD)
        rows = slice(h * ROWS, (h + 1) * ROWS)
        q_nope = q_ref[:, base : base + NOPE]
        absorbed = lax.dot_general(q_nope, wuk_ref[:, h * NOPE : (h + 1) * NOPE], NT, preferred_element_type=f32)
        qf[rows, :KVL] = absorbed.astype(bf16)
        roped = rotate(q_ref[:, base + NOPE : base + NOPE + RD].astype(f32), cos_q, sin_q)
        qf[rows, KVL:] = jnp.concatenate([roped, feature], axis=1).astype(bf16)
    m_s[...] = jnp.full(m_s.shape, HIDDEN_MASK, f32)
    l_s[...] = jnp.zeros(l_s.shape, f32)
    acc[...] = jnp.zeros(acc.shape, f32)

    key_first = pl.multiple_of(c * 64 + zh * 16, 16)
    cos_k, sin_k = rope_tables(pos_ref[pl.ds(key_first, 16), :])
    seg_k = seg_ref[pl.ds(key_first, 16), :]
    lane_k = lax.broadcasted_iota(jnp.int32, (16, RD), 1)
    feature_k = jnp.where((lane_k == 0) & (seg_k == 1), 1.0, 0.0)
    for copy in rs:
        copy.wait()
    latent = tot[zh] + rs_recv[0] + rs_recv[1] + rs_recv[2]
    compressed = latent[:, :KVL]
    mean_square = jnp.mean(compressed * compressed, axis=-1, keepdims=True)
    normed = (compressed * lax.rsqrt(mean_square + NORM_EPS) * gain_ref[...]).astype(bf16)
    key_a[zh, x, c, y, zl] = normed[:, :256]
    key_b[zh, x, c, y, zl] = normed[:, 256:]
    key_c[zh, x, c, y, zl] = jnp.concatenate(
        [rotate(latent[:, KVL : KVL + RD], cos_k, sin_k), feature_k], axis=1
    ).astype(bf16)

    keys = (key_a, key_b, key_c)
    ag = []
    for k in (1, 2, 3):
        for i, key in enumerate(keys):
            ref = key.at[zh, x, c, y, zl]
            ag.append(remote(ref, ref, s_ag.at[k - 1, i], r_ag.at[k - 1, i], place(x, y, z + 4 * k, c)))
    for copy in ag:
        copy.start()

    def toward(axis, step):
        if axis == 0:
            return place(x + step, y, z, c)
        if axis == 1:
            return place(x, y + step, z, c)
        return place(x, y, z + {1: 1, 2: 2, 3: -1}[step], c)

    def phase1(m):
        copies = []
        for i, axis in enumerate((2, 2, 0)):
            ref = keys[i].at[m, x, c, y, zl]
            for k, step in enumerate(RING):
                copies.append(remote(ref, ref, s_p1.at[m, i * 3 + k], r_p1.at[m, i * 3 + k], toward(axis, step)))
        return copies

    def phase2(m):
        refs = (key_a.at[m, x, c, y], key_b.at[m, x, c, y], key_c.at[m, :, c, y, zl])
        copies = []
        for i, axis in enumerate((1, 0, 1)):
            for k, step in enumerate(RING):
                copies.append(
                    remote(refs[i], refs[i], s_p2.at[m, i * 3 + k], r_p2.at[m, i * 3 + k], toward(axis, step))
                )
        return copies

    def planes(m, d):
        return (
            key_a.at[m, (x + d) % 4, c],
            key_b.at[m, :, c, (y + d) % 4],
            key_c.at[m, :, c, :, (zl + d) % 4],
        )

    def halves(m, d, first):
        part = pl.ds(0, 2) if first else pl.ds(2, 2)
        return (
            key_a.at[m, (x + d) % 4, c, part],
            key_b.at[m, part, c, (y + d) % 4],
            key_c.at[m, part, c, :, (zl + d) % 4],
        )

    def phase3(m):
        refs = planes(m, 0)
        copies = []
        for i in range(3):
            for k, step in enumerate((1, 3)):
                copies.append(
                    remote(refs[i], refs[i], s_p3.at[m, i * 2 + k], r_p3.at[m, i * 2 + k], toward(i, step))
                )
        return copies

    def forward(m):
        copies = []
        for k, (step, back, first) in enumerate(((1, 3, True), (3, 1, False))):
            refs = halves(m, back, first)
            for i in range(3):
                copies.append(
                    remote(refs[i], refs[i], s_hf.at[m, i * 2 + k], r_hf.at[m, i * 2 + k], toward(i, step))
                )
        return copies

    def share(m, d):
        refs = planes(m, d)
        return [remote(refs[i], refs[i], s_sh.at[m, d * 3 + i], r_sh.at[m, d * 3 + i], sib) for i in range(3)]

    def start(copies):
        for copy in copies:
            copy.start()

    def wait_recv(copies):
        for copy in copies:
            copy.wait_recv()

    def wait_send(copies):
        for copy in copies:
            copy.wait_send()

    qloc = (y * 4 + zl) * ROWS

    def unit(m, xq, diagonal):
        ka = key_a[m, xq].reshape(512, 256)
        kb = key_b[m, xq].reshape(512, 256)
        kc = key_c[m, xq].reshape(512, 128)
        s = lax.dot_general(qf[...], jnp.concatenate([ka, kb, kc], axis=1), NT, preferred_element_type=f32)
        if diagonal:
            n = lax.broadcasted_iota(jnp.int32, (1, 512), 1)
            key_at = ((n >> 4) & 15) * ROWS + (n >> 8) * 64 + m * 16 + (n & 15)
            query_at = (lax.broadcasted_iota(jnp.int32, (HEADS * ROWS, 1), 0) & (ROWS - 1)) + qloc
            s = jnp.where(key_at <= query_at, s, HIDDEN_MASK)
        old = m_s[...]
        new = jnp.maximum(old, jnp.max(s, axis=1, keepdims=True))
        shrink = jnp.exp2((old - new) * EXP_SCALE)
        p = jnp.exp2((s - jnp.concatenate([new] * 4, axis=1)) * EXP_SCALE)
        l_s[...] = l_s[...] * shrink + (p[:, :128] + p[:, 128:256] + p[:, 256:384] + p[:, 384:])
        m_s[...] = new
        weights = p.astype(bf16)
        shrink = jnp.concatenate([shrink, shrink], axis=1)
        acc[:, :256] = acc[:, :256] * shrink + jnp.dot(weights, ka, preferred_element_type=f32)
        acc[:, 256:] = acc[:, 256:] * shrink + jnp.dot(weights, kb, preferred_element_type=f32)

    def attend(m):
        def full(xq, carry):
            unit(m, xq, False)
            return carry

        lax.fori_loop(0, x, full, 0)
        unit(m, x, True)

    wait_recv(ag)

    def loop(body):
        lax.fori_loop(0, 4, lambda m, carry: (body(m), carry)[1], 0)

    loop(lambda m: start(phase1(m)))

    def second(m):
        wait_recv(phase1(m))
        start(phase2(m))

    loop(second)

    def third(m):
        wait_recv(phase2(m))
        start(share(m, 0))

        @pl.when(m == 0)
        def _():
            start(phase3(m))

    loop(third)

    def stage(m, carry):
        @pl.when(m < 4)
        def _():
            wait_recv(phase3(m))

            @pl.when(m < 3)
            def _():
                start(phase3(m + 1))

            start(forward(m))
            start(share(m, 1))
            start(share(m, 3))

        @pl.when((m >= 1) & (m <= 4))
        def _():
            wait_recv(forward(m - 1))
            start(share(m - 1, 2))

        @pl.when(m >= 2)
        def _():
            for d in range(4):
                wait_recv(share(m - 2, d))
            attend(m - 2)

        return carry

    lax.fori_loop(0, 6, stage, 0)

    total = jnp.sum(l_s[...], axis=1, keepdims=True)
    for h in range(HEADS):
        rows = slice(h * ROWS, (h + 1) * ROWS)
        mixed = (acc[rows, :] / total[rows, :]).astype(bf16)
        out_ref[:, h * VD : (h + 1) * VD] = jnp.dot(
            mixed, wuv_ref[:, h * VD : (h + 1) * VD], preferred_element_type=f32
        ).astype(bf16)

    wait_send(ag)

    def finish(m):
        wait_send(phase1(m))
        wait_send(phase2(m))
        wait_send(phase3(m))
        wait_send(forward(m))
        for d in range(4):
            wait_send(share(m, d))

    loop(finish)


def shards(hidden, w_dkv, kv_gain, w_uk, w_uv, queries, segments, positions):
    f32, bf16 = jnp.float32, jnp.bfloat16
    dma = pltpu.SemaphoreType.DMA
    keys = (4, 4, 2, 4, 4, 16)
    vmem = pl.BlockSpec(memory_space=pltpu.VMEM)
    sems = [dma, dma, dma((3,)), dma((3,)), dma((3, 3)), dma((3, 3))]
    for count in (9, 9, 6, 6, 12):
        sems += [dma((4, count)), dma((4, count))]
    return pl.pallas_call(
        kernel,
        out_shape=jax.ShapeDtypeStruct((ROWS, HEADS * VD), bf16),
        in_specs=[vmem] * 8,
        out_specs=vmem,
        scratch_shapes=[
            pltpu.VMEM((64, 640), f32),
            pltpu.VMEM((64, 640), f32),
            pltpu.VMEM((4, 16, 640), f32),
            pltpu.VMEM((3, 16, 640), f32),
            pltpu.VMEM((*keys, 256), bf16),
            pltpu.VMEM((*keys, 256), bf16),
            pltpu.VMEM((*keys, 128), bf16),
            pltpu.VMEM((HEADS * ROWS, 640), bf16),
            pltpu.VMEM((HEADS * ROWS, KVL), f32),
            pltpu.VMEM((HEADS * ROWS, 128), f32),
            pltpu.VMEM((HEADS * ROWS, 128), f32),
            *sems,
        ],
        compiler_params=pltpu.CompilerParams(
            collective_id=0, has_side_effects=True, vmem_limit_bytes=56 * 2**20
        ),
    )(
        hidden, w_dkv, kv_gain.reshape(1, KVL), w_uk, w_uv, queries,
        positions.reshape(ROWS, 1), segments.reshape(ROWS, 1),
    )


def solution(mesh):
    in_specs = (
        P("ctx", "head"),
        P("head", None),
        P(),
        P(None, "head"),
        P(None, "head"),
        P("ctx", "head"),
        P("ctx"),
        P("ctx"),
    )
    out_specs = P("ctx", "head")
    return jax.shard_map(shards, mesh=mesh, in_specs=in_specs, out_specs=out_specs, check_vma=False)
```

```python
import functools
import math

import jax
import jax.numpy as jnp
from jax import lax
from jax.experimental import pallas as pl
from jax.experimental.pallas import tpu as pltpu
from jax.sharding import PartitionSpec as P

KVL = 512
RD = 64
NOPE = 128
VD = 128
ROPE_BASE = 10000.0
NORM_EPS = 1e-06
ROWS = 128
HEADS = 6
HIDDEN_MASK = -1e30
EXP_SCALE = math.log2(math.e) / math.sqrt(NOPE + RD)
MESH = pl.DeviceIdType.MESH
NT = (((1,), (1,)), ((), ()))
RING = (1, 3, 2)
WIDTH = 640


def place(x, y, z, core):
    x, y, z = (x + 8) % 4, (y + 8) % 4, (z + 32) % 16
    return (x * 16 + y * 4 + z % 4, (z // 4) * 2 + core)


def remote(src, dst, send, recv, device):
    return pltpu.make_async_remote_copy(
        src_ref=src, dst_ref=dst, send_sem=send, recv_sem=recv, device_id=device, device_id_type=MESH
    )


def rope_tables(pos):
    lane = lax.broadcasted_iota(jnp.int32, (1, RD), 1)
    half = (lane % (RD // 2)).astype(jnp.float32)
    frequency = jnp.exp(half * (-2.0 * math.log(ROPE_BASE) / RD))
    angles = pos.astype(jnp.float32) * frequency
    sign = jnp.where(lane < RD // 2, -1.0, 1.0)
    return jnp.cos(angles), jnp.sin(angles) * sign


def rotate(v, cosine, sine):
    swapped = jnp.concatenate([v[:, RD // 2 :], v[:, : RD // 2]], axis=1)
    return v * cosine + swapped * sine


def column(row):
    n = row.shape[1]
    at = lax.broadcasted_iota(jnp.int32, (n, n), 0) == lax.broadcasted_iota(jnp.int32, (n, n), 1)
    return jnp.sum(jnp.where(at, row.astype(jnp.float32), 0.0), axis=1, keepdims=True)


def kernel(
    hid_hbm, wd_hbm, gain_ref, wuk_hbm, wuv_hbm, q_hbm, pos_ref, seg_ref, out_ref,
    hid_ref, wd_ref, wuk_ref, wuv_ref, q_ref, pos_s, seg_s,
    lat_send, lat_recv, tot, rs_recv, keys, qf, acc, m_s, l_s,
    s_in, s_sib, r_sib, s_rs, r_rs, s_ag, r_ag, s_p1, r_p1, s_p2, r_p2, s_p3, r_p3, s_fw, r_fw, s_sh, r_sh,
):
    ctx, head = lax.axis_index("ctx"), lax.axis_index("head")
    x, y, zl = ctx // 16, (ctx // 4) % 4, ctx % 4
    zh, c = head // 2, head % 2
    z = zh * 4 + zl
    sib = place(x, y, z, 1 - c)
    f32, bf16 = jnp.float32, jnp.bfloat16

    loads = [
        pltpu.make_async_copy(src, dst, s_in.at[i])
        for i, (src, dst) in enumerate(
            ((hid_hbm, hid_ref), (wd_hbm, wd_ref), (q_hbm, q_ref), (wuk_hbm, wuk_ref), (wuv_hbm, wuv_ref))
        )
    ]
    for load in loads:
        load.start()

    barrier = pltpu.get_barrier_semaphore()
    offsets = [(1, 0, 0), (2, 0, 0), (3, 0, 0), (0, 1, 0), (0, 2, 0), (0, 3, 0)]
    offsets += [(0, 0, k) for k in (1, -1, 2, -2, 4, 8, 12)]
    pl.semaphore_signal(barrier, inc=1, device_id=sib, device_id_type=MESH)
    for dx, dy, dz in offsets:
        pl.semaphore_signal(barrier, inc=1, device_id=place(x + dx, y + dy, z + dz, c), device_id_type=MESH)

    def partial(first):
        return lax.dot_general(hid_ref[pl.ds(first, 64), :], wd_ref[...], NT, preferred_element_type=f32)

    other = pl.multiple_of((1 - c) * 64, 64)
    mine = pl.multiple_of(c * 64, 64)
    lat_send[:, KVL + RD :] = jnp.zeros((64, 64), f32)
    loads[0].wait()
    loads[1].wait()
    lat_send[:, : KVL + RD] = partial(other)
    pl.semaphore_wait(barrier, 1 + len(offsets))
    swap = remote(lat_send, lat_recv, s_sib, r_sib, sib)
    swap.start()
    own = jnp.concatenate([partial(mine), jnp.zeros((64, 64), f32)], axis=1)
    swap.wait()
    tot[...] = (own + lat_recv[...]).reshape(4, 16, WIDTH)

    rs = [
        remote(tot.at[(zh + k) % 4], rs_recv.at[k - 1], s_rs.at[k - 1], r_rs.at[k - 1], place(x, y, z + 4 * k, c))
        for k in (1, 2, 3)
    ]
    for copy in rs:
        copy.start()

    pos_s[...] = column(pos_ref[...])
    seg_s[...] = column(seg_ref[...])
    cos_q, sin_q = rope_tables(pos_s[...])
    lane = lax.broadcasted_iota(jnp.int32, (ROWS, RD), 1)
    feature = jnp.where((lane == 0) & (seg_s[...] == 2.0), HIDDEN_MASK, 0.0)
    loads[2].wait()
    loads[3].wait()
    for h in range(HEADS):
        base = h * (NOPE + RD)
        rows = slice(h * ROWS, (h + 1) * ROWS)
        q_nope = q_ref[:, base : base + NOPE]
        absorbed = lax.dot_general(q_nope, wuk_ref[:, h * NOPE : (h + 1) * NOPE], NT, preferred_element_type=f32)
        qf[rows, :KVL] = absorbed.astype(bf16)
        roped = rotate(q_ref[:, base + NOPE : base + NOPE + RD].astype(f32), cos_q, sin_q)
        qf[rows, KVL:] = jnp.concatenate([roped, feature], axis=1).astype(bf16)
    m_s[...] = jnp.full(m_s.shape, HIDDEN_MASK, f32)
    l_s[...] = jnp.zeros(l_s.shape, f32)
    acc[...] = jnp.zeros(acc.shape, f32)

    key_first = pl.multiple_of(c * 64 + zh * 16, 16)
    cos_k, sin_k = rope_tables(pos_s[pl.ds(key_first, 16), :])
    seg_k = seg_s[pl.ds(key_first, 16), :]
    lane_k = lax.broadcasted_iota(jnp.int32, (16, RD), 1)
    feature_k = jnp.where((lane_k == 0) & (seg_k == 1.0), 1.0, 0.0)
    for copy in rs:
        copy.wait()
    latent = tot[zh] + rs_recv[0] + rs_recv[1] + rs_recv[2]
    compressed = latent[:, :KVL]
    mean_square = jnp.mean(compressed * compressed, axis=-1, keepdims=True)
    normed = compressed * lax.rsqrt(mean_square + NORM_EPS) * gain_ref[...]
    roped_k = rotate(latent[:, KVL : KVL + RD], cos_k, sin_k)
    keys[zh, x, c, y, zl] = jnp.concatenate([normed, roped_k, feature_k], axis=1).astype(bf16)

    piece = keys.at[zh, x, c, y, zl]
    ag = [remote(piece, piece, s_ag.at[k - 1], r_ag.at[k - 1], place(x, y, z + 4 * k, c)) for k in (1, 2, 3)]
    for copy in ag:
        copy.start()

    def toward(axis, step):
        if axis == 0:
            return place(x + step, y, z, c)
        if axis == 1:
            return place(x, y + step, z, c)
        return place(x, y, z + {1: 1, 2: 2, 3: -1}[step], c)

    first_axis, second_axis = (2, 0, 1), (1, 2, 0)
    block = {
        0: lambda m: keys.at[m, x, c, y],
        1: lambda m: keys.at[m, :, c, y, zl],
        2: lambda m: keys.at[m, x, c, :, zl],
    }
    plane = {
        0: lambda m, d, part: keys.at[m, (x + d) % 4, c, part],
        1: lambda m, d, part: keys.at[m, part, c, (y + d) % 4],
        2: lambda m, d, part: keys.at[m, part, c, :, (zl + d) % 4],
    }
    low, high, whole = pl.ds(0, 2), pl.ds(2, 2), pl.ds(0, 4)

    def phase1(kind, m):
        ref = keys.at[m, x, c, y, zl]
        return [
            remote(ref, ref, s_p1.at[m, k], r_p1.at[m, k], toward(first_axis[kind], step))
            for k, step in enumerate(RING)
        ]

    def phase2(kind, m):
        ref = block[kind](m)
        return [
            remote(ref, ref, s_p2.at[m, k], r_p2.at[m, k], toward(second_axis[kind], step))
            for k, step in enumerate(RING)
        ]

    def phase3(kind, m, turn):
        copies = []
        for k, (step, parts) in enumerate(((1, (low, high)), (3, (high, low)))):
            ref = plane[kind](m, 0, parts[turn])
            copies.append(remote(ref, ref, s_p3.at[m, k * 2 + turn], r_p3.at[m, k * 2 + turn], toward(kind, step)))
        return copies

    def forward(kind, m):
        copies = []
        for k, (step, back, part) in enumerate(((1, 3, low), (3, 1, high))):
            ref = plane[kind](m, back, part)
            copies.append(remote(ref, ref, s_fw.at[m, k], r_fw.at[m, k], toward(kind, step)))
        return copies

    def share(kind, m, d):
        ref = plane[kind](m, d, whole)
        return [remote(ref, ref, s_sh.at[m, d], r_sh.at[m, d], sib)]

    def start(copies):
        for copy in copies:
            copy.start()

    def wait_recv(copies):
        for copy in copies:
            copy.wait_recv()

    def wait_send(copies):
        for copy in copies:
            copy.wait_send()

    def each(task, *sets):
        for m in sets:
            if m < 3:
                task(m, m)
            else:
                for kind in (0, 1):
                    pl.when(c == kind)(functools.partial(task, kind, m))

    def one(kind, m):
        start(phase1(kind, m))

    def two(kind, m):
        wait_recv(phase1(kind, m))
        start(phase2(kind, m))

    def three(kind, m):
        wait_recv(phase2(kind, m))
        start(share(kind, m, 0))
        if m < 3:
            four(kind, m)

    def four(kind, m):
        start(phase3(kind, m, 0))
        start(phase3(kind, m, 1))

    def five(kind, m):
        wait_recv(phase3(kind, m, 0))
        start(forward(kind, m))

    def six(kind, m):
        wait_recv(phase3(kind, m, 1))
        start(share(kind, m, 1))
        start(share(kind, m, 3))

    def seven(kind, m):
        wait_recv(forward(kind, m))
        start(share(kind, m, 2))

    query_at = (lax.broadcasted_iota(jnp.int32, (HEADS * ROWS, 1), 0) & (ROWS - 1)) + ctx * ROWS
    n = lax.broadcasted_iota(jnp.int32, (1, 512), 1)

    def unit(k, key_at):
        s = lax.dot_general(qf[...], k, NT, preferred_element_type=f32)
        s = jnp.where(key_at <= query_at, s, HIDDEN_MASK)
        old = m_s[...]
        new = jnp.maximum(old, jnp.max(s, axis=1, keepdims=True))
        shrink = jnp.exp2((old - new) * EXP_SCALE)
        p = jnp.exp2((s - jnp.concatenate([new] * 4, axis=1)) * EXP_SCALE)
        l_s[...] = l_s[...] * shrink + (p[:, :128] + p[:, 128:256] + p[:, 256:384] + p[:, 384:])
        m_s[...] = new
        update = jnp.dot(p.astype(bf16), k[:, :KVL], preferred_element_type=f32)
        acc[...] = acc[...] * jnp.concatenate([shrink] * 4, axis=1) + update

    def unit_x(m, xq):
        @pl.when(xq <= x)
        def _():
            at = (xq * 16 + ((n >> 4) & 15)) * ROWS + (n >> 8) * 64 + m * 16 + (n & 15)
            unit(keys[m, xq].reshape(512, WIDTH), at)

    def unit_y(m, yq):
        at = ((n >> 7) * 16 + yq * 4 + ((n >> 4) & 3)) * ROWS + ((n >> 6) & 1) * 64 + m * 16 + (n & 15)
        unit(keys[m, :, :, yq].reshape(512, WIDTH), at)

    def unit_z(m, zq):
        at = ((n >> 7) * 16 + ((n >> 4) & 3) * 4 + zq) * ROWS + ((n >> 6) & 1) * 64 + m * 16 + (n & 15)
        unit(keys[m, :, :, :, zq].reshape(512, WIDTH), at)

    wait_recv(ag)
    each(one, 0, 1, 2, 3)
    each(two, 0, 1, 2, 3)
    each(three, 0, 1, 2, 3)

    def step(t, carry):
        d = jnp.where(t < 2, t, 5 - t)
        joint = t < 4

        @pl.when(t == 1)
        def _():
            each(five, 0, 1, 2)
            each(six, 0, 1, 2)
            each(four, 3)

        @pl.when(t == 2)
        def _():
            each(seven, 0, 1, 2)

        @pl.when(t == 3)
        def _():
            each(six, 3)

        @pl.when(t == 4)
        def _():
            for k in range(4):
                wait_recv(share(0, 3, k))

        @pl.when(joint)
        def _():
            wait_recv(share(0, 0, d))

        unit_x(jnp.where(joint, 0, 3), jnp.where(joint, (x + d) % 4, t - 4))

        @pl.when(joint)
        def _():
            wait_recv(share(1, 1, d))
            unit_y(1, (y + d) % 4)

            @pl.when(t == 2)
            def _():
                each(five, 3)

            @pl.when(t == 3)
            def _():
                each(seven, 3)

            wait_recv(share(2, 2, d))
            unit_z(2, (zl + d) % 4)

        return carry

    lax.fori_loop(0, 8, step, 0)

    loads[4].wait()
    total = jnp.sum(l_s[...], axis=1, keepdims=True)
    for h in range(HEADS):
        rows = slice(h * ROWS, (h + 1) * ROWS)
        mixed = (acc[rows, :] / total[rows, :]).astype(bf16)
        out_ref[:, h * VD : (h + 1) * VD] = jnp.dot(
            mixed, wuv_ref[:, h * VD : (h + 1) * VD], preferred_element_type=f32
        ).astype(bf16)

    wait_send(ag)

    def finish(kind, m):
        wait_send(phase1(kind, m) + phase2(kind, m) + phase3(kind, m, 0) + phase3(kind, m, 1) + forward(kind, m))
        for d in range(4):
            wait_send(share(kind, m, d))

    each(finish, 0, 1, 2, 3)


def shards(hidden, w_dkv, kv_gain, w_uk, w_uv, queries, segments, positions):
    f32, bf16 = jnp.float32, jnp.bfloat16
    dma = pltpu.SemaphoreType.DMA
    vmem = pl.BlockSpec(memory_space=pltpu.VMEM)
    hbm = pl.BlockSpec(memory_space=pl.ANY)
    sems = [dma((5,)), dma, dma, dma((3,)), dma((3,)), dma((3,)), dma((3,))]
    for count in (3, 3, 4, 2, 4):
        sems += [dma((4, count)), dma((4, count))]
    operands = (hidden, w_dkv.T, w_uk, w_uv, queries)
    return pl.pallas_call(
        kernel,
        out_shape=jax.ShapeDtypeStruct((ROWS, HEADS * VD), bf16),
        in_specs=[hbm, hbm, vmem, hbm, hbm, hbm, vmem, vmem],
        out_specs=vmem,
        scratch_shapes=[
            *[pltpu.VMEM(a.shape, a.dtype) for a in operands],
            pltpu.VMEM((ROWS, 1), f32),
            pltpu.VMEM((ROWS, 1), f32),
            pltpu.VMEM((64, WIDTH), f32),
            pltpu.VMEM((64, WIDTH), f32),
            pltpu.VMEM((4, 16, WIDTH), f32),
            pltpu.VMEM((3, 16, WIDTH), f32),
            pltpu.VMEM((4, 4, 2, 4, 4, 16, WIDTH), bf16),
            pltpu.VMEM((HEADS * ROWS, WIDTH), bf16),
            pltpu.VMEM((HEADS * ROWS, KVL), f32),
            pltpu.VMEM((HEADS * ROWS, 128), f32),
            pltpu.VMEM((HEADS * ROWS, 128), f32),
            *sems,
        ],
        compiler_params=pltpu.CompilerParams(
            collective_id=0, has_side_effects=True, vmem_limit_bytes=56 * 2**20
        ),
    )(
        operands[0], operands[1], kv_gain.reshape(1, KVL), *operands[2:],
        positions.reshape(1, ROWS), segments.reshape(1, ROWS),
    )


def solution(mesh):
    in_specs = (
        P("ctx", "head"),
        P("head", None),
        P(),
        P(None, "head"),
        P(None, "head"),
        P("ctx", "head"),
        P("ctx"),
        P("ctx"),
    )
    out_specs = P("ctx", "head")
    return jax.shard_map(shards, mesh=mesh, in_specs=in_specs, out_specs=out_specs, check_vma=False)
```

```python
import functools
import math

import jax
import jax.numpy as jnp
from jax import lax
from jax.experimental import pallas as pl
from jax.experimental.pallas import tpu as pltpu
from jax.sharding import PartitionSpec as P

KVL = 512
RD = 64
NOPE = 128
VD = 128
ROPE_BASE = 10000.0
NORM_EPS = 1e-06
ROWS = 128
HEADS = 6
HIDDEN_MASK = -1e30
EXP_SCALE = math.log2(math.e) / math.sqrt(NOPE + RD)
MESH = pl.DeviceIdType.MESH
NT = (((1,), (1,)), ((), ()))
RING = (1, 3, 2)
WIDTH = 640


def place(x, y, z, core):
    x, y, z = (x + 8) % 4, (y + 8) % 4, (z + 32) % 16
    return (x * 16 + y * 4 + z % 4, (z // 4) * 2 + core)


def remote(src, dst, send, recv, device):
    return pltpu.make_async_remote_copy(
        src_ref=src, dst_ref=dst, send_sem=send, recv_sem=recv, device_id=device, device_id_type=MESH
    )


def rope_tables(pos):
    lane = lax.broadcasted_iota(jnp.int32, (1, RD), 1)
    half = (lane % (RD // 2)).astype(jnp.float32)
    frequency = jnp.exp(half * (-2.0 * math.log(ROPE_BASE) / RD))
    angles = pos.astype(jnp.float32) * frequency
    sign = jnp.where(lane < RD // 2, -1.0, 1.0)
    return jnp.cos(angles), jnp.sin(angles) * sign


def rotate(v, cosine, sine):
    swapped = jnp.concatenate([v[:, RD // 2 :], v[:, : RD // 2]], axis=1)
    return v * cosine + swapped * sine


def column(row):
    n = row.shape[1]
    at = lax.broadcasted_iota(jnp.int32, (n, n), 0) == lax.broadcasted_iota(jnp.int32, (n, n), 1)
    return jnp.sum(jnp.where(at, row.astype(jnp.float32), 0.0), axis=1, keepdims=True)


def kernel(
    hid_hbm, wd_hbm, gain_hbm, wuk_hbm, wuv_hbm, q_hbm, pos_hbm, seg_hbm, out_ref,
    hid_ref, wd_ref, wuk_ref, wuv_ref, q_ref, gain_ref, pos_ref, seg_ref, pos_s, seg_s,
    lat_send, lat_recv, tot, tot_rope, rs_recv, rs_rope, keys, qf, acc, m_s, l_s,
    s_in, s_sib, r_sib, s_rs, r_rs, s_ag, r_ag, s_p1, r_p1, s_p2, r_p2, s_p3, r_p3, s_fw, r_fw, s_sh, r_sh,
):
    ctx, head = lax.axis_index("ctx"), lax.axis_index("head")
    x, y, zl = ctx // 16, (ctx // 4) % 4, ctx % 4
    zh, c = head // 2, head % 2
    z = zh * 4 + zl
    sib = place(x, y, z, 1 - c)
    f32, bf16 = jnp.float32, jnp.bfloat16

    loads = [
        pltpu.make_async_copy(src, dst, s_in.at[i])
        for i, (src, dst) in enumerate(
            (
                (hid_hbm, hid_ref), (q_hbm, q_ref), (wuk_hbm, wuk_ref), (wuv_hbm, wuv_ref),
                (gain_hbm, gain_ref), (pos_hbm, pos_ref), (seg_hbm, seg_ref),
            )
        )
    ]
    first_loads = [
        pltpu.make_async_copy(wd_hbm.at[pl.ds(144 * i, 144)], wd_ref.at[pl.ds(144 * i, 144)], s_in.at[7 + i]) for i in range(4)
    ]
    for load in loads[:1] + first_loads:
        load.start()

    barrier = pltpu.get_barrier_semaphore()
    offsets = [(1, 0, 0), (2, 0, 0), (3, 0, 0), (0, 1, 0), (0, 2, 0), (0, 3, 0)]
    offsets += [(0, 0, k) for k in (1, -1, 2, -2, 4, 8, 12)]
    pl.semaphore_signal(barrier, inc=1, device_id=sib, device_id_type=MESH)
    for dx, dy, dz in offsets:
        pl.semaphore_signal(barrier, inc=1, device_id=place(x + dx, y + dy, z + dz, c), device_id_type=MESH)

    def partial(first):
        return lax.dot_general(hid_ref[pl.ds(first, 64), :], wd_ref[...], NT, preferred_element_type=f32)

    other = pl.multiple_of((1 - c) * 64, 64)
    mine = pl.multiple_of(c * 64, 64)
    lat_send[:, KVL + RD :] = jnp.zeros((64, 64), f32)
    loads[0].wait()
    for load in first_loads:
        load.wait()
    lat_send[:, : KVL + RD] = partial(other)
    pl.semaphore_wait(barrier, 1 + len(offsets))
    swap = remote(lat_send, lat_recv, s_sib, r_sib, sib)
    swap.start()
    for load in loads[1:]:
        load.start()
    own = jnp.concatenate([partial(mine), jnp.zeros((64, 64), f32)], axis=1)
    swap.wait()
    total_rows = own + lat_recv[...]
    tot[...] = total_rows[:, :KVL].reshape(4, 16, KVL)
    for i in range(4):
        rope_rows = total_rows[i * 16 : (i + 1) * 16, KVL : KVL + RD]
        tot_rope[i] = jnp.concatenate([rope_rows[:8], rope_rows[8:]], axis=1)

    rs = []
    for k in (1, 2, 3):
        for i, (src, dst) in enumerate(((tot, rs_recv), (tot_rope, rs_rope))):
            peer = place(x, y, z + 4 * k, c)
            rs.append(remote(src.at[(zh + k) % 4], dst.at[k - 1], s_rs.at[k - 1, i], r_rs.at[k - 1, i], peer))
    for copy in rs:
        copy.start()

    for load in loads[4:]:
        load.wait()
    pos_s[...] = column(pos_ref[...])
    seg_s[...] = column(seg_ref[...])
    key_first = pl.multiple_of(c * 64 + zh * 16, 16)
    cos_k, sin_k = rope_tables(pos_s[pl.ds(key_first, 16), :])
    seg_k = seg_s[pl.ds(key_first, 16), :]
    lane_k = lax.broadcasted_iota(jnp.int32, (16, RD), 1)
    feature_k = jnp.where((lane_k == 0) & (seg_k == 1.0), 1.0, 0.0)
    for copy in rs:
        copy.wait()
    compressed = tot[zh] + rs_recv[0] + rs_recv[1] + rs_recv[2]
    rope_k = tot_rope[zh] + rs_rope[0] + rs_rope[1] + rs_rope[2]
    rope_k = jnp.concatenate([rope_k[:, :RD], rope_k[:, RD:]], axis=0)
    mean_square = jnp.mean(compressed * compressed, axis=-1, keepdims=True)
    normed = compressed * lax.rsqrt(mean_square + NORM_EPS) * gain_ref[...]
    roped_k = rotate(rope_k, cos_k, sin_k)
    keys[zh, x, c, y, zl] = jnp.concatenate([normed, roped_k, feature_k], axis=1).astype(bf16)

    piece = keys.at[zh, x, c, y, zl]
    ag = [remote(piece, piece, s_ag.at[k - 1], r_ag.at[k - 1], place(x, y, z + 4 * k, c)) for k in (1, 2, 3)]
    for copy in ag:
        copy.start()

    cos_q, sin_q = rope_tables(pos_s[...])
    lane = lax.broadcasted_iota(jnp.int32, (ROWS, RD), 1)
    feature = jnp.where((lane == 0) & (seg_s[...] == 2.0), HIDDEN_MASK, 0.0)
    loads[1].wait()
    loads[2].wait()
    for h in range(HEADS):
        base = h * (NOPE + RD)
        rows = slice(h * ROWS, (h + 1) * ROWS)
        q_nope = q_ref[:, base : base + NOPE]
        absorbed = lax.dot_general(q_nope, wuk_ref[:, h * NOPE : (h + 1) * NOPE], NT, preferred_element_type=f32)
        qf[rows, :KVL] = absorbed.astype(bf16)
        roped = rotate(q_ref[:, base + NOPE : base + NOPE + RD].astype(f32), cos_q, sin_q)
        qf[rows, KVL:] = jnp.concatenate([roped, feature], axis=1).astype(bf16)
    m_s[...] = jnp.full(m_s.shape, HIDDEN_MASK, f32)
    l_s[...] = jnp.zeros(l_s.shape, f32)
    acc[...] = jnp.zeros(acc.shape, f32)

    across = jnp.where(zl % 2 == 0, 2, -2)

    def toward(axis, step):
        if axis == 0:
            return place(x + step, y, z, c)
        if axis == 1:
            return place(x, y + step, z, c)
        return place(x, y, z + {1: 1, 2: across, 3: -1}[step], c)

    first_axis, second_axis = (2, 0, 1), (1, 2, 0)
    block = {
        0: lambda m: keys.at[m, x, c, y],
        1: lambda m: keys.at[m, :, c, y, zl],
        2: lambda m: keys.at[m, x, c, :, zl],
    }
    plane = {
        0: lambda m, d, part: keys.at[m, (x + d) % 4, c, part],
        1: lambda m, d, part: keys.at[m, part, c, (y + d) % 4],
        2: lambda m, d, part: keys.at[m, part, c, :, (zl + d) % 4],
    }
    low, high, whole = pl.ds(0, 2), pl.ds(2, 2), pl.ds(0, 4)

    def route(kind, m):
        if (kind, m) == (0, 3):
            return 1, 2, block[2](m)
        return first_axis[kind], second_axis[kind], block[kind](m)

    def phase1(kind, m):
        ref = keys.at[m, x, c, y, zl]
        return [
            remote(ref, ref, s_p1.at[m, k], r_p1.at[m, k], toward(route(kind, m)[0], step))
            for k, step in enumerate(RING)
        ]

    def phase2(kind, m):
        _, axis, ref = route(kind, m)
        return [
            remote(ref, ref, s_p2.at[m, k], r_p2.at[m, k], toward(axis, step))
            for k, step in enumerate(RING)
        ]

    def phase3(kind, m, turn):
        copies = []
        for k, (step, parts) in enumerate(((1, (low, high)), (3, (high, low)))):
            ref = plane[kind](m, 0, parts[turn])
            copies.append(remote(ref, ref, s_p3.at[m, k * 2 + turn], r_p3.at[m, k * 2 + turn], toward(kind, step)))
        return copies

    def forward(kind, m):
        copies = []
        for k, (step, back, part) in enumerate(((1, 3, low), (3, 1, high))):
            ref = plane[kind](m, back, part)
            copies.append(remote(ref, ref, s_fw.at[m, k], r_fw.at[m, k], toward(kind, step)))
        return copies

    def share(kind, m, d):
        ref = plane[kind](m, d, whole)
        return [remote(ref, ref, s_sh.at[m, d], r_sh.at[m, d], sib)]

    def start(copies):
        for copy in copies:
            copy.start()

    def wait_recv(copies):
        for copy in copies:
            copy.wait_recv()

    def wait_send(copies):
        for copy in copies:
            copy.wait_send()

    def each(task, *sets):
        for m in sets:
            if m < 3:
                task(m, m)
            else:
                for kind in (0, 1):
                    pl.when(c == kind)(functools.partial(task, kind, m))

    def one(kind, m):
        start(phase1(kind, m))

    def two(kind, m):
        wait_recv(phase1(kind, m))
        start(phase2(kind, m))

    def three(kind, m):
        wait_recv(phase2(kind, m))
        start(share(kind, m, 0))
        if m < 3:
            four(kind, m)

    def four(kind, m):
        start(phase3(kind, m, 0))
        start(phase3(kind, m, 1))

    def five(kind, m):
        wait_recv(phase3(kind, m, 0))
        start(forward(kind, m))

    def six(kind, m):
        wait_recv(phase3(kind, m, 1))
        start(share(kind, m, 1))
        start(share(kind, m, 3))

    def seven(kind, m):
        wait_recv(forward(kind, m))
        start(share(kind, m, 2))

    query_at = (lax.broadcasted_iota(jnp.int32, (HEADS * ROWS, 1), 0) & (ROWS - 1)) + ctx * ROWS
    n = lax.broadcasted_iota(jnp.int32, (1, 512), 1)

    def unit(k, key_at):
        s = lax.dot_general(qf[...], k, NT, preferred_element_type=f32)
        s = jnp.where(key_at <= query_at, s, HIDDEN_MASK)
        old = m_s[...]
        new = jnp.maximum(old, jnp.max(s, axis=1, keepdims=True))
        shrink = jnp.exp2((old - new) * EXP_SCALE)
        p = jnp.exp2((s - jnp.concatenate([new] * 4, axis=1)) * EXP_SCALE)
        l_s[...] = l_s[...] * shrink + (p[:, :128] + p[:, 128:256] + p[:, 256:384] + p[:, 384:])
        m_s[...] = new
        update = jnp.dot(p.astype(bf16), k[:, :KVL], preferred_element_type=f32)
        acc[...] = acc[...] * jnp.concatenate([shrink] * 4, axis=1) + update

    def unit_x(m, xq):
        @pl.when(xq <= x)
        def _():
            at = (xq * 16 + ((n >> 4) & 15)) * ROWS + (n >> 8) * 64 + m * 16 + (n & 15)
            unit(keys[m, xq].reshape(512, WIDTH), at)

    def unit_y(m, yq):
        at = ((n >> 7) * 16 + yq * 4 + ((n >> 4) & 3)) * ROWS + ((n >> 6) & 1) * 64 + m * 16 + (n & 15)
        unit(keys[m, :, :, yq].reshape(512, WIDTH), at)

    def unit_z(m, zq):
        at = ((n >> 7) * 16 + ((n >> 4) & 3) * 4 + zq) * ROWS + ((n >> 6) & 1) * 64 + m * 16 + (n & 15)
        unit(keys[m, :, :, :, zq].reshape(512, WIDTH), at)

    def unit_3(d):
        xq, yq = (x + d) % 4, (y + d) % 4
        half = n & 255
        at_0 = (xq * 16 + (half >> 4)) * ROWS
        at_1 = ((half >> 6) * 16 + yq * 4 + ((half >> 4) & 3)) * ROWS + 64
        k = jnp.concatenate([keys[3, xq, 0].reshape(256, WIDTH), keys[3, :, 1, yq].reshape(256, WIDTH)], axis=0)
        unit(k, jnp.where(n < 256, at_0, at_1) + 3 * 16 + (n & 15))

    wait_recv(ag)
    each(one, 0, 1, 2, 3)
    each(two, 0, 1, 2, 3)
    each(three, 0, 1, 2, 3)

    wait_recv(share(0, 0, 0))
    unit_x(0, (x + 0) % 4)
    wait_recv(share(1, 1, 0))
    unit_y(1, (y + 0) % 4)
    wait_recv(share(2, 2, 0))
    unit_z(2, (zl + 0) % 4)
    each(five, 0, 1, 2)
    each(four, 3)
    wait_recv(share(0, 3, 0))
    unit_3(0)
    each(six, 0, 1, 2)
    wait_recv(share(0, 0, 1))
    unit_x(0, (x + 1) % 4)
    wait_recv(share(1, 1, 1))
    unit_y(1, (y + 1) % 4)
    wait_recv(share(2, 2, 1))
    unit_z(2, (zl + 1) % 4)
    each(five, 3)
    wait_recv(share(0, 0, 3))
    unit_x(0, (x + 3) % 4)
    each(seven, 0, 1, 2)
    wait_recv(share(1, 1, 3))
    unit_y(1, (y + 3) % 4)
    each(six, 3)
    wait_recv(share(2, 2, 3))
    unit_z(2, (zl + 3) % 4)
    wait_recv(share(0, 0, 2))
    unit_x(0, (x + 2) % 4)
    wait_recv(share(1, 1, 2))
    unit_y(1, (y + 2) % 4)
    each(seven, 3)
    wait_recv(share(2, 2, 2))
    unit_z(2, (zl + 2) % 4)
    wait_recv(share(0, 3, 1))
    unit_3(1)
    wait_recv(share(0, 3, 3))
    unit_3(3)
    wait_recv(share(0, 3, 2))
    unit_3(2)

    loads[3].wait()
    inverse = 1.0 / jnp.sum(l_s[...], axis=1, keepdims=True)
    for h in range(HEADS):
        rows = slice(h * ROWS, (h + 1) * ROWS)
        mixed = (acc[rows, :] * inverse[rows, :]).astype(bf16)
        out_ref[:, h * VD : (h + 1) * VD] = jnp.dot(
            mixed, wuv_ref[:, h * VD : (h + 1) * VD], preferred_element_type=f32
        ).astype(bf16)

    wait_send(ag)

    def finish(kind, m):
        wait_send(phase1(kind, m) + phase2(kind, m) + phase3(kind, m, 0) + phase3(kind, m, 1) + forward(kind, m))
        for d in range(4):
            wait_send(share(kind, m, d))

    each(finish, 0, 1, 2, 3)


def shards(hidden, w_dkv, kv_gain, w_uk, w_uv, queries, segments, positions):
    f32, bf16 = jnp.float32, jnp.bfloat16
    dma = pltpu.SemaphoreType.DMA
    vmem = pl.BlockSpec(memory_space=pltpu.VMEM)
    hbm = pl.BlockSpec(memory_space=pl.ANY)
    sems = [dma((11,)), dma, dma, dma((3, 2)), dma((3, 2)), dma((3,)), dma((3,))]
    for count in (3, 3, 4, 2, 4):
        sems += [dma((4, count)), dma((4, count))]
    operands = (hidden, w_dkv.T, w_uk, w_uv, queries)
    return pl.pallas_call(
        kernel,
        out_shape=jax.ShapeDtypeStruct((ROWS, HEADS * VD), bf16),
        in_specs=[hbm] * 8,
        out_specs=vmem,
        scratch_shapes=[
            *[pltpu.VMEM(a.shape, a.dtype) for a in operands],
            pltpu.VMEM((1, KVL), f32),
            pltpu.VMEM((1, ROWS), jnp.int32),
            pltpu.VMEM((1, ROWS), jnp.int32),
            pltpu.VMEM((ROWS, 1), f32),
            pltpu.VMEM((ROWS, 1), f32),
            pltpu.VMEM((64, WIDTH), f32),
            pltpu.VMEM((64, WIDTH), f32),
            pltpu.VMEM((4, 16, KVL), f32),
            pltpu.VMEM((4, 8, 2 * RD), f32),
            pltpu.VMEM((3, 16, KVL), f32),
            pltpu.VMEM((3, 8, 2 * RD), f32),
            pltpu.VMEM((4, 4, 2, 4, 4, 16, WIDTH), bf16),
            pltpu.VMEM((HEADS * ROWS, WIDTH), bf16),
            pltpu.VMEM((HEADS * ROWS, KVL), f32),
            pltpu.VMEM((HEADS * ROWS, 128), f32),
            pltpu.VMEM((HEADS * ROWS, 128), f32),
            *sems,
        ],
        compiler_params=pltpu.CompilerParams(
            collective_id=0, has_side_effects=True, vmem_limit_bytes=56 * 2**20
        ),
    )(
        operands[0], operands[1], kv_gain.reshape(1, KVL), *operands[2:],
        positions.reshape(1, ROWS), segments.reshape(1, ROWS),
    )


def solution(mesh):
    in_specs = (
        P("ctx", "head"),
        P("head", None),
        P(),
        P(None, "head"),
        P(None, "head"),
        P("ctx", "head"),
        P("ctx"),
        P("ctx"),
    )
    out_specs = P("ctx", "head")
    return jax.shard_map(shards, mesh=mesh, in_specs=in_specs, out_specs=out_specs, check_vma=False)
```

```python
import functools
import math

import jax
import jax.numpy as jnp
from jax import lax
from jax.experimental import pallas as pl
from jax.experimental.pallas import tpu as pltpu
from jax.sharding import PartitionSpec as P

KVL = 512
RD = 64
NOPE = 128
VD = 128
ROPE_BASE = 10000.0
NORM_EPS = 1e-06
ROWS = 128
HEADS = 6
HIDDEN_MASK = -1e30
EXP_SCALE = math.log2(math.e) / math.sqrt(NOPE + RD)
MESH = pl.DeviceIdType.MESH
NT = (((1,), (1,)), ((), ()))
RING = (1, 3, 2)
WIDTH = 640


def place(x, y, z, core):
    x, y, z = (x + 8) % 4, (y + 8) % 4, (z + 32) % 16
    return (x * 16 + y * 4 + z % 4, (z // 4) * 2 + core)


def remote(src, dst, send, recv, device):
    return pltpu.make_async_remote_copy(
        src_ref=src, dst_ref=dst, send_sem=send, recv_sem=recv, device_id=device, device_id_type=MESH
    )


def rope_tables(pos):
    lane = lax.broadcasted_iota(jnp.int32, (1, RD), 1)
    half = (lane % (RD // 2)).astype(jnp.float32)
    frequency = jnp.exp(half * (-2.0 * math.log(ROPE_BASE) / RD))
    angles = pos.astype(jnp.float32) * frequency
    sign = jnp.where(lane < RD // 2, -1.0, 1.0)
    return jnp.cos(angles), jnp.sin(angles) * sign


def rotate(v, cosine, sine):
    swapped = jnp.concatenate([v[:, RD // 2 :], v[:, : RD // 2]], axis=1)
    return v * cosine + swapped * sine


def column(row):
    n = row.shape[1]
    at = lax.broadcasted_iota(jnp.int32, (n, n), 0) == lax.broadcasted_iota(jnp.int32, (n, n), 1)
    return jnp.sum(jnp.where(at, row.astype(jnp.float32), 0.0), axis=1, keepdims=True)


def kernel(
    hid_hbm, wd_hbm, gain_hbm, wuk_hbm, wuv_hbm, q_hbm, pos_hbm, seg_hbm, out_ref,
    hid_ref, wd_ref, wuk_ref, wuv_ref, q_ref, gain_ref, pos_ref, seg_ref, pos_s, seg_s,
    lat_send, lat_recv, tot, tot_rope, rs_recv, rs_rope, keys, qf, acc, m_s, l_s,
    s_in, s_sib, r_sib, s_rs, r_rs, s_ag, r_ag, s_p1, r_p1, s_p2, r_p2, s_p3, r_p3, s_fw, r_fw, s_sh, r_sh,
):
    ctx, head = lax.axis_index("ctx"), lax.axis_index("head")
    x, y, zl = ctx // 16, (ctx // 4) % 4, ctx % 4
    zh, c = head // 2, head % 2
    z = zh * 4 + zl
    sib = place(x, y, z, 1 - c)
    f32, bf16 = jnp.float32, jnp.bfloat16

    loads = [
        pltpu.make_async_copy(src, dst, s_in.at[i])
        for i, (src, dst) in enumerate(
            (
                (hid_hbm, hid_ref), (q_hbm, q_ref), (wuk_hbm, wuk_ref), (wuv_hbm, wuv_ref),
                (gain_hbm, gain_ref), (pos_hbm, pos_ref), (seg_hbm, seg_ref),
            )
        )
    ]
    first_loads = [
        pltpu.make_async_copy(wd_hbm.at[pl.ds(144 * i, 144)], wd_ref.at[pl.ds(144 * i, 144)], s_in.at[7 + i]) for i in range(4)
    ]
    for load in loads[:1] + first_loads:
        load.start()

    barrier = pltpu.get_barrier_semaphore()
    offsets = [(1, 0, 0), (2, 0, 0), (3, 0, 0), (0, 1, 0), (0, 2, 0), (0, 3, 0)]
    offsets += [(0, 0, k) for k in (1, -1, 2, -2, 4, 8, 12)]
    pl.semaphore_signal(barrier, inc=1, device_id=sib, device_id_type=MESH)
    for dx, dy, dz in offsets:
        pl.semaphore_signal(barrier, inc=1, device_id=place(x + dx, y + dy, z + dz, c), device_id_type=MESH)

    def partial(first):
        return lax.dot_general(hid_ref[pl.ds(first, 64), :], wd_ref[...], NT, preferred_element_type=f32)

    other = pl.multiple_of((1 - c) * 64, 64)
    mine = pl.multiple_of(c * 64, 64)
    lat_send[:, KVL + RD :] = jnp.zeros((64, 64), f32)
    loads[0].wait()
    for load in first_loads:
        load.wait()
    lat_send[:, : KVL + RD] = partial(other)
    pl.semaphore_wait(barrier, 1 + len(offsets))
    swap = remote(lat_send, lat_recv, s_sib, r_sib, sib)
    swap.start()
    for load in loads[1:]:
        load.start()
    own = jnp.concatenate([partial(mine), jnp.zeros((64, 64), f32)], axis=1)
    swap.wait()
    total_rows = own + lat_recv[...]
    tot[...] = total_rows[:, :KVL].reshape(4, 16, KVL)
    for i in range(4):
        rope_rows = total_rows[i * 16 : (i + 1) * 16, KVL : KVL + RD]
        tot_rope[i] = jnp.concatenate([rope_rows[:8], rope_rows[8:]], axis=1)

    rs = []
    for k in (1, 2, 3):
        for i, (src, dst) in enumerate(((tot, rs_recv), (tot_rope, rs_rope))):
            peer = place(x, y, z + 4 * k, c)
            rs.append(remote(src.at[(zh + k) % 4], dst.at[k - 1], s_rs.at[k - 1, i], r_rs.at[k - 1, i], peer))
    for copy in rs:
        copy.start()

    for load in loads[4:]:
        load.wait()
    pos_s[...] = column(pos_ref[...])
    seg_s[...] = column(seg_ref[...])
    key_first = pl.multiple_of(c * 64 + zh * 16, 16)
    cos_k, sin_k = rope_tables(pos_s[pl.ds(key_first, 16), :])
    seg_k = seg_s[pl.ds(key_first, 16), :]
    lane_k = lax.broadcasted_iota(jnp.int32, (16, RD), 1)
    feature_k = jnp.where((lane_k == 0) & (seg_k == 1.0), 1.0, 0.0)
    for copy in rs:
        copy.wait()
    compressed = tot[zh] + rs_recv[0] + rs_recv[1] + rs_recv[2]
    rope_k = tot_rope[zh] + rs_rope[0] + rs_rope[1] + rs_rope[2]
    rope_k = jnp.concatenate([rope_k[:, :RD], rope_k[:, RD:]], axis=0)
    mean_square = jnp.mean(compressed * compressed, axis=-1, keepdims=True)
    normed = compressed * lax.rsqrt(mean_square + NORM_EPS) * gain_ref[...]
    roped_k = rotate(rope_k, cos_k, sin_k)
    keys[zh, x, c, y, zl] = jnp.concatenate([normed, roped_k, feature_k], axis=1).astype(bf16)

    piece = keys.at[zh, x, c, y, zl]
    ag = [remote(piece, piece, s_ag.at[k - 1], r_ag.at[k - 1], place(x, y, z + 4 * k, c)) for k in (1, 2, 3)]
    for copy in ag:
        copy.start()

    cos_q, sin_q = rope_tables(pos_s[...])
    lane = lax.broadcasted_iota(jnp.int32, (ROWS, RD), 1)
    feature = jnp.where((lane == 0) & (seg_s[...] == 2.0), HIDDEN_MASK, 0.0)
    loads[1].wait()
    loads[2].wait()
    for h in range(HEADS):
        base = h * (NOPE + RD)
        rows = slice(h * ROWS, (h + 1) * ROWS)
        q_nope = q_ref[:, base : base + NOPE]
        absorbed = lax.dot_general(q_nope, wuk_ref[:, h * NOPE : (h + 1) * NOPE], NT, preferred_element_type=f32)
        qf[rows, :KVL] = absorbed.astype(bf16)
        roped = rotate(q_ref[:, base + NOPE : base + NOPE + RD].astype(f32), cos_q, sin_q)
        qf[rows, KVL:] = jnp.concatenate([roped, feature], axis=1).astype(bf16)
    m_s[...] = jnp.full(m_s.shape, HIDDEN_MASK, f32)
    l_s[...] = jnp.zeros(l_s.shape, f32)
    acc[...] = jnp.zeros(acc.shape, f32)

    across = jnp.where(zl % 2 == 0, 2, -2)

    def toward(axis, step):
        if axis == 0:
            return place(x + step, y, z, c)
        if axis == 1:
            return place(x, y + step, z, c)
        return place(x, y, z + {1: 1, 2: across, 3: -1}[step], c)

    first_axis, second_axis = (2, 0, 1), (1, 2, 0)
    block = {
        0: lambda m: keys.at[m, x, c, y],
        1: lambda m: keys.at[m, :, c, y, zl],
        2: lambda m: keys.at[m, x, c, :, zl],
    }
    plane = {
        0: lambda m, d, part: keys.at[m, (x + d) % 4, c, part],
        1: lambda m, d, part: keys.at[m, part, c, (y + d) % 4],
        2: lambda m, d, part: keys.at[m, part, c, :, (zl + d) % 4],
    }
    low, high, whole = pl.ds(0, 2), pl.ds(2, 2), pl.ds(0, 4)

    def route(kind, m):
        if (kind, m) == (0, 3):
            return 1, 2, block[2](m)
        if (kind, m) == (1, 3):
            return 2, 0, block[0](m)
        return first_axis[kind], second_axis[kind], block[kind](m)

    def phase1(kind, m):
        ref = keys.at[m, x, c, y, zl]
        return [
            remote(ref, ref, s_p1.at[m, k], r_p1.at[m, k], toward(route(kind, m)[0], step))
            for k, step in enumerate(RING)
        ]

    def phase2(kind, m):
        _, axis, ref = route(kind, m)
        return [
            remote(ref, ref, s_p2.at[m, k], r_p2.at[m, k], toward(axis, step))
            for k, step in enumerate(RING)
        ]

    def phase3(kind, m, turn):
        copies = []
        for k, (step, parts) in enumerate(((1, (low, high)), (3, (high, low)))):
            ref = plane[kind](m, 0, parts[turn])
            copies.append(remote(ref, ref, s_p3.at[m, k * 2 + turn], r_p3.at[m, k * 2 + turn], toward(kind, step)))
        return copies

    def forward(kind, m):
        copies = []
        for k, (step, back, part) in enumerate(((1, 3, low), (3, 1, high))):
            ref = plane[kind](m, back, part)
            copies.append(remote(ref, ref, s_fw.at[m, k], r_fw.at[m, k], toward(kind, step)))
        return copies

    def share(kind, m, d):
        ref = plane[kind](m, d, whole)
        return [remote(ref, ref, s_sh.at[m, d], r_sh.at[m, d], sib)]

    def start(copies):
        for copy in copies:
            copy.start()

    def wait_recv(copies):
        for copy in copies:
            copy.wait_recv()

    def wait_send(copies):
        for copy in copies:
            copy.wait_send()

    def each(task, *sets):
        for m in sets:
            if m < 3:
                task(m, m)
            else:
                for kind in (0, 1):
                    pl.when(c == kind)(functools.partial(task, kind, m))

    def one(kind, m):
        start(phase1(kind, m))

    def two(kind, m):
        wait_recv(phase1(kind, m))
        start(phase2(kind, m))

    def three(kind, m):
        wait_recv(phase2(kind, m))
        start(share(kind, m, 0))
        if m < 3:
            four(kind, m)

    def four(kind, m):
        start(phase3(kind, m, 0))
        start(phase3(kind, m, 1))

    def five(kind, m):
        wait_recv(phase3(kind, m, 0))
        start(forward(kind, m))

    def six(kind, m):
        wait_recv(phase3(kind, m, 1))
        start(share(kind, m, 1))
        start(share(kind, m, 3))

    def seven(kind, m):
        wait_recv(forward(kind, m))
        start(share(kind, m, 2))

    query_at = (lax.broadcasted_iota(jnp.int32, (HEADS * ROWS, 1), 0) & (ROWS - 1)) + ctx * ROWS
    n = lax.broadcasted_iota(jnp.int32, (1, 512), 1)

    def unit(k, key_at):
        s = lax.dot_general(qf[...], k, NT, preferred_element_type=f32)
        s = jnp.where(key_at <= query_at, s, HIDDEN_MASK)
        old = m_s[...]
        new = jnp.maximum(old, jnp.max(s, axis=1, keepdims=True))
        shrink = jnp.exp2((old - new) * EXP_SCALE)
        p = jnp.exp2((s - jnp.concatenate([new] * 4, axis=1)) * EXP_SCALE)
        l_s[...] = l_s[...] * shrink + (p[:, :128] + p[:, 128:256] + p[:, 256:384] + p[:, 384:])
        m_s[...] = new
        update = jnp.dot(p.astype(bf16), k[:, :KVL], preferred_element_type=f32)
        acc[...] = acc[...] * jnp.concatenate([shrink] * 4, axis=1) + update

    def unit_x(m, xq):
        @pl.when(xq <= x)
        def _():
            at = (xq * 16 + ((n >> 4) & 15)) * ROWS + (n >> 8) * 64 + m * 16 + (n & 15)
            unit(keys[m, xq].reshape(512, WIDTH), at)

    def unit_y(m, yq):
        at = ((n >> 7) * 16 + yq * 4 + ((n >> 4) & 3)) * ROWS + ((n >> 6) & 1) * 64 + m * 16 + (n & 15)
        unit(keys[m, :, :, yq].reshape(512, WIDTH), at)

    def unit_z(m, zq):
        at = ((n >> 7) * 16 + ((n >> 4) & 3) * 4 + zq) * ROWS + ((n >> 6) & 1) * 64 + m * 16 + (n & 15)
        unit(keys[m, :, :, :, zq].reshape(512, WIDTH), at)

    def unit_3(d):
        xq, yq = (x + d) % 4, (y + d) % 4
        half = n & 255
        at_0 = (xq * 16 + (half >> 4)) * ROWS
        at_1 = ((half >> 6) * 16 + yq * 4 + ((half >> 4) & 3)) * ROWS + 64
        k = jnp.concatenate([keys[3, xq, 0].reshape(256, WIDTH), keys[3, :, 1, yq].reshape(256, WIDTH)], axis=0)
        unit(k, jnp.where(n < 256, at_0, at_1) + 3 * 16 + (n & 15))

    wait_recv(ag)
    each(one, 0, 1, 2, 3)
    each(two, 0, 1, 2, 3)
    each(three, 0, 1, 2)

    def step(t, carry):
        d = jnp.where(t < 2, t, 5 - t)
        wait_recv(share(0, 0, d))
        unit_x(0, (x + d) % 4)

        @pl.when(t == 0)
        def _():
            each(three, 3)

        @pl.when(t == 2)
        def _():
            each(seven, 0, 1, 2)

        wait_recv(share(1, 1, d))
        unit_y(1, (y + d) % 4)

        @pl.when(t == 2)
        def _():
            each(six, 3)

        @pl.when(t == 3)
        def _():
            each(seven, 3)

        wait_recv(share(2, 2, d))
        unit_z(2, (zl + d) % 4)

        @pl.when(t == 0)
        def _():
            each(five, 0, 1, 2)
            each(four, 3)

        @pl.when(t == 1)
        def _():
            each(five, 3)

        def last(i, carry):
            d = jnp.where(t == 0, 0, jnp.where(i < 1, 1, 4 - i))
            wait_recv(share(0, 3, d))
            unit_3(d)
            return carry

        lax.fori_loop(0, jnp.where(t == 0, 1, jnp.where(t == 3, 3, 0)), last, 0)

        @pl.when(t == 0)
        def _():
            each(six, 0, 1, 2)

        return carry

    lax.fori_loop(0, 4, step, 0)

    loads[3].wait()
    inverse = 1.0 / jnp.sum(l_s[...], axis=1, keepdims=True)
    for h in range(HEADS):
        rows = slice(h * ROWS, (h + 1) * ROWS)
        mixed = (acc[rows, :] * inverse[rows, :]).astype(bf16)
        out_ref[:, h * VD : (h + 1) * VD] = jnp.dot(
            mixed, wuv_ref[:, h * VD : (h + 1) * VD], preferred_element_type=f32
        ).astype(bf16)

    wait_send(ag)

    def finish(kind, m):
        wait_send(phase1(kind, m) + phase2(kind, m) + phase3(kind, m, 0) + phase3(kind, m, 1) + forward(kind, m))
        for d in range(4):
            wait_send(share(kind, m, d))

    each(finish, 0, 1, 2, 3)


def shards(hidden, w_dkv, kv_gain, w_uk, w_uv, queries, segments, positions):
    f32, bf16 = jnp.float32, jnp.bfloat16
    dma = pltpu.SemaphoreType.DMA
    vmem = pl.BlockSpec(memory_space=pltpu.VMEM)
    hbm = pl.BlockSpec(memory_space=pl.ANY)
    sems = [dma((11,)), dma, dma, dma((3, 2)), dma((3, 2)), dma((3,)), dma((3,))]
    for count in (3, 3, 4, 2, 4):
        sems += [dma((4, count)), dma((4, count))]
    operands = (hidden, w_dkv.T, w_uk, w_uv, queries)
    return pl.pallas_call(
        kernel,
        out_shape=jax.ShapeDtypeStruct((ROWS, HEADS * VD), bf16),
        in_specs=[hbm] * 8,
        out_specs=vmem,
        scratch_shapes=[
            *[pltpu.VMEM(a.shape, a.dtype) for a in operands],
            pltpu.VMEM((1, KVL), f32),
            pltpu.VMEM((1, ROWS), jnp.int32),
            pltpu.VMEM((1, ROWS), jnp.int32),
            pltpu.VMEM((ROWS, 1), f32),
            pltpu.VMEM((ROWS, 1), f32),
            pltpu.VMEM((64, WIDTH), f32),
            pltpu.VMEM((64, WIDTH), f32),
            pltpu.VMEM((4, 16, KVL), f32),
            pltpu.VMEM((4, 8, 2 * RD), f32),
            pltpu.VMEM((3, 16, KVL), f32),
            pltpu.VMEM((3, 8, 2 * RD), f32),
            pltpu.VMEM((4, 4, 2, 4, 4, 16, WIDTH), bf16),
            pltpu.VMEM((HEADS * ROWS, WIDTH), bf16),
            pltpu.VMEM((HEADS * ROWS, KVL), f32),
            pltpu.VMEM((HEADS * ROWS, 128), f32),
            pltpu.VMEM((HEADS * ROWS, 128), f32),
            *sems,
        ],
        compiler_params=pltpu.CompilerParams(
            collective_id=0, has_side_effects=True, vmem_limit_bytes=56 * 2**20
        ),
    )(
        operands[0], operands[1], kv_gain.reshape(1, KVL), *operands[2:],
        positions.reshape(1, ROWS), segments.reshape(1, ROWS),
    )


def solution(mesh):
    in_specs = (
        P("ctx", "head"),
        P("head", None),
        P(),
        P(None, "head"),
        P(None, "head"),
        P("ctx", "head"),
        P("ctx"),
        P("ctx"),
    )
    out_specs = P("ctx", "head")
    return jax.shard_map(shards, mesh=mesh, in_specs=in_specs, out_specs=out_specs, check_vma=False)
```
